32 devices in a mesh: groups: 2 (over x), region: 16 (over z, y, core).
Axes of the slice: x: 2, y: 2, z: 4, core: 2. Of those that a mesh axis runs over, the one named last changes fastest.
Arguments:
- grid_latent: bfloat16 [32768, 512], P(('groups', 'region')), parts along dimension 0, may hold values from -6 to 6
- grid_slot: int32 [32768], P(('groups', 'region')), parts along dimension 0, may hold values from 0 to 1535, as said below
- mesh_latent: bfloat16 [4096, 512], P(('groups', 'region')), parts along dimension 0, may hold values from -6 to 6
- link_target: int32 [2, 49152], P(None, ('groups', 'region')), parts along dimension 1, may hold values from 0 to 128, as said below
- grid_weight: bfloat16 [512, 512], replicated, may hold values from -0.25 to 0.25
- mesh_weight: bfloat16 [512, 512], replicated, may hold values from -0.25 to 0.25
- link_bias: float32 [512], replicated, may hold values from -4 to 4
- link_weight: bfloat16 [512, 512], replicated, may hold values from -0.25 to 0.25
- link_gain: float32 [512], replicated, may hold values from 0.1 to 1.9
- edge_sender: int32 [16384], P(('groups', 'region')), parts along dimension 0, may hold values from 0 to 191, as said below
- edge_receiver: int32 [16384], P(('groups', 'region')), parts along dimension 0, may hold values from 0 to 127
- halo_list: int32 [64, 32], P(('groups', 'region')), parts along dimension 0, may hold values from 0 to 127
- sender_weight: bfloat16 [512, 512], replicated, may hold values from -0.25 to 0.25
- receiver_weight: bfloat16 [512, 512], replicated, may hold values from -0.25 to 0.25
- edge_bias: float32 [512], replicated, may hold values from -4 to 4
- edge_weight: bfloat16 [512, 512], replicated, may hold values from -0.25 to 0.25
- cotangent: bfloat16 [4096, 512], P(('groups', 'region')), parts along dimension 0, may hold values from -6 to 6
Outputs:
- mesh_next: bfloat16 [4096, 512], P(('groups', 'region')), parts along dimension 0
- mesh_grad: bfloat16 [4096, 512], P(('groups', 'region')), parts along dimension 0
The draws below stay inside these ranges and needn't reach their ends.
There are 2 independent parts, one for each index of `groups`. The reference program is written for one: setup_inputs(seed, part) draws one part's arguments, and reference() takes and returns one part's arrays. A program takes and returns all parts, laid end to end along the dimension named above; an argument that names none is the same for every part. Nothing has to cross between parts.
Inputs may be any that keep to these rules, and one draw needn't show every extreme that they name: `grid_slot`: within the nodes of one band the slots are distinct; slot p binds the node to region p // 96. In every draw some region takes 96 nodes from every band. `link_target`: column d * 1536 + s * 96 + c holds 128 exactly where no node of band s took slot d * 96 + c, else a mesh node of region d. `edge_sender`: in each region the first 384 edges have a sender below 128, the last 128 one of 128 or more; the first region takes no sender from below, the last none from above.
All inputs are finite; a program needn't handle non-finite values.
Results may differ from the reference program's by a relative error of at most 0.0077.
Values may be sent and summed in bfloat16 or wider, within the bound.
A program may use at most 64 MiB of HBM per device.

```python
import jax
import jax.numpy as jnp
from jax import lax

D = 512
GD = 1024
MD = 128
ED = 512
HN = 32
SLOT_DEV = 1536
CAP = 96
GRID = 16384
MESH = 2048
MESH_EDGES = 8192
N_REGION = 16


def layout_tables(key):
    region_count = N_REGION
    count_of_slots = SLOT_DEV
    slot_limit = SLOT_DEV // N_REGION
    busiest_region = jax.random.randint(jax.random.fold_in(key, 11), (), 0, region_count)
    order_keys = jax.random.split(jax.random.fold_in(key, 12), region_count)
    rank_positions = jax.vmap(lambda one_key: jax.random.permutation(one_key, count_of_slots))(order_keys)
    reward_extra = jnp.where(jnp.arange(count_of_slots) // slot_limit == busiest_region, count_of_slots, 0)
    region_rating = rank_positions + reward_extra[None, :]
    chosen = jnp.argsort(-region_rating, axis=1)[:, :GD]
    mix_keys = jax.random.split(jax.random.fold_in(key, 13), region_count)
    shuffle = jax.vmap(lambda one_key: jax.random.permutation(one_key, GD))(mix_keys)
    chosen = jnp.take_along_axis(chosen, shuffle, axis=1).astype(jnp.int32)
    filled = jnp.zeros((region_count, count_of_slots), jnp.int32).at[jnp.arange(region_count)[:, None], chosen].set(1)
    return (chosen, filled)


def draw_grid_slot(key, part):
    chosen, filled = layout_tables(key)
    return chosen.reshape(-1).astype(jnp.int32)


def draw_link_target(key, part):
    chosen, filled = layout_tables(key)
    key = jax.random.fold_in(key, 5)
    slot_limit = SLOT_DEV // N_REGION
    targets = jax.random.randint(key, (2, N_REGION, N_REGION, slot_limit), 0, MD)
    arrived = filled.reshape(N_REGION, N_REGION, slot_limit).transpose(1, 0, 2)
    result = jnp.where(arrived[None] == 1, targets, MD)
    return result.reshape(2, N_REGION * SLOT_DEV).astype(jnp.int32)


def draw_edge_sender(key, part):
    key = jax.random.fold_in(key, 7)
    key_inner, key_rows, key_side = jax.random.split(key, 3)
    total = N_REGION * ED
    position = jnp.arange(total, dtype=jnp.int32)
    edge_region = position // ED
    within = position % ED
    local_pick = jax.random.randint(key_inner, (total,), 0, MD)
    halo_pick = jax.random.randint(key_rows, (total,), 0, HN)
    side = jax.random.randint(key_side, (total,), 0, 2)
    side = jnp.where(edge_region == 0, 1, jnp.where(edge_region == N_REGION - 1, 0, side))
    return jnp.where(within < ED - ED // 4, local_pick, MD + side * HN + halo_pick).astype(jnp.int32)


def place_ends(drawn, key, low, high):
    index_at = [jax.random.randint(jax.random.fold_in(key, axis), (), 0, length) for axis, length in enumerate(drawn.shape)]
    main_axis = drawn.shape.index(max(drawn.shape))
    neighbour = index_at[:main_axis] + [(index_at[main_axis] + 1) % drawn.shape[main_axis]] + index_at[main_axis + 1:]
    return drawn.at[tuple(index_at)].set(low).at[tuple(neighbour)].set(high)


def block_levels(key, shape, cuts, smallest, top_value):
    def one(dim, shards_of):
        steps = jax.random.uniform(jax.random.fold_in(jax.random.fold_in(key, 6), dim), (shards_of,), jnp.float32, smallest / len(cuts), top_value / len(cuts))
        return jnp.repeat(jnp.exp(steps), shape[dim] // shards_of).reshape((-1,) + (1,) * (len(shape) - dim - 1))

    level = one(*cuts[0])
    for cut in cuts[1:]:
        level = level * one(*cut)
    return level


def normal_values(own_key, extent, scale, reach, cuts=(), kind=jnp.bfloat16):
    values = scale * jax.random.normal(own_key, extent, jnp.float32)
    if cuts:
        values = values * block_levels(own_key, extent, cuts, -0.22, 0.18)
    return jnp.clip(values, -reach, reach).astype(kind)


def setup_inputs(seed: int = 0, part: int = 0) -> dict:
    keys = jax.random.split(jax.random.key(seed), 18)
    own_keys = jax.random.split(jax.random.fold_in(keys[17], part), 18)
    grid_latent = normal_values(own_keys[0], (GRID, D), 1.0, 6.0, ((0, 16),))
    grid_slot = draw_grid_slot(jax.random.fold_in(jax.random.fold_in(keys[17], part), 71), part)
    mesh_latent = normal_values(own_keys[2], (MESH, D), 1.0, 6.0, ((0, 16),))
    link_target = draw_link_target(jax.random.fold_in(jax.random.fold_in(keys[17], part), 71), part)
    grid_weight = normal_values(keys[4], (D, D), D ** -0.5, 0.25)
    mesh_weight = normal_values(keys[5], (D, D), D ** -0.5, 0.25)
    link_bias = normal_values(keys[6], (D,), 1.0, 4.0, (), jnp.float32)
    link_weight = normal_values(keys[7], (D, D), D ** -0.5, 0.25)
    link_gain = jnp.clip(1.0 + 0.18 * jax.random.normal(keys[8], (D,), jnp.float32), 0.1, 1.9)
    edge_sender = draw_edge_sender(jax.random.fold_in(jax.random.fold_in(keys[17], part), 71), part)
    edge_receiver = place_ends(jax.random.randint(own_keys[10], (MESH_EDGES,), 0, MD), jax.random.fold_in(own_keys[10], 1), 0, MD - 1).astype(jnp.int32)
    halo_list = place_ends(jax.random.randint(own_keys[11], (2 * N_REGION, HN), 0, MD), jax.random.fold_in(own_keys[11], 1), 0, MD - 1).astype(jnp.int32)
    sender_weight = normal_values(keys[12], (D, D), D ** -0.5, 0.25)
    receiver_weight = normal_values(keys[13], (D, D), D ** -0.5, 0.25)
    edge_bias = normal_values(keys[14], (D,), 1.0, 4.0, (), jnp.float32)
    edge_weight = normal_values(keys[15], (D, D), D ** -0.5, 0.25)
    cotangent = normal_values(own_keys[16], (MESH, D), 1.0, 6.0, ((0, 16),))
    return dict(grid_latent=grid_latent, grid_slot=grid_slot, mesh_latent=mesh_latent, link_target=link_target, grid_weight=grid_weight, mesh_weight=mesh_weight, link_bias=link_bias, link_weight=link_weight, link_gain=link_gain, edge_sender=edge_sender, edge_receiver=edge_receiver, halo_list=halo_list, sender_weight=sender_weight, receiver_weight=receiver_weight, edge_bias=edge_bias, edge_weight=edge_weight, cotangent=cotangent)


def layer_norm(values, gain):
    centred = values - lax.optimization_barrier(jnp.mean(values, axis=-1, keepdims=True))
    spread = lax.optimization_barrier(jnp.mean(centred * centred, axis=-1, keepdims=True))
    return centred * lax.rsqrt(spread + 1e-05) * gain

def silu_slope(values):
    sigmoid = jax.nn.sigmoid(values)
    return sigmoid * (1.0 + values * (1.0 - sigmoid))

def reference(grid_latent, grid_slot, mesh_latent, link_target, grid_weight, mesh_weight, link_bias, link_weight, link_gain, edge_sender, edge_receiver, halo_list, sender_weight, receiver_weight, edge_bias, edge_weight, cotangent):
    band_index = jnp.arange(GRID, dtype=jnp.int32) // GD
    region = grid_slot // CAP
    column = region * SLOT_DEV + band_index * CAP + grid_slot % CAP
    local_target = link_target[:, column]
    present = (local_target < MD).astype(jnp.float32)
    target = region[None, :] * MD + jnp.minimum(local_target, MD - 1)
    grid_projected = jnp.dot(grid_latent, grid_weight, preferred_element_type=jnp.float32).astype(jnp.bfloat16)
    mesh_projected = jnp.dot(mesh_latent, mesh_weight, preferred_element_type=jnp.float32)
    totals = jnp.zeros((MESH, D), jnp.float32)
    for branch in range(2):
        hidden = jax.nn.silu(grid_projected.astype(jnp.float32) + mesh_projected[target[branch]] + link_bias).astype(jnp.bfloat16)
        output = jnp.dot(hidden, link_weight, preferred_element_type=jnp.float32)
        message = layer_norm(output, link_gain) * present[branch][:, None]
        totals = totals + jax.ops.segment_sum(message, target[branch], num_segments=MESH)
    mesh_mid = (mesh_latent.astype(jnp.float32) + totals).astype(jnp.bfloat16)
    edge_region = jnp.arange(MESH_EDGES, dtype=jnp.int32) // ED
    receiver = edge_region * MD + edge_receiver
    lower_owner = jnp.clip(edge_region - 1, 0, N_REGION - 1)
    upper_owner = jnp.clip(edge_region + 1, 0, N_REGION - 1)
    from_lower = lower_owner * MD + halo_list[2 * lower_owner + 1, jnp.clip(edge_sender - MD, 0, HN - 1)]
    from_upper = upper_owner * MD + halo_list[2 * upper_owner, jnp.clip(edge_sender - MD - HN, 0, HN - 1)]
    sender = jnp.where(edge_sender < MD, edge_region * MD + edge_sender, jnp.where(edge_sender < MD + HN, from_lower, from_upper))
    sender_projected = jnp.dot(mesh_mid, sender_weight, preferred_element_type=jnp.float32)
    receiver_projected = jnp.dot(mesh_mid, receiver_weight, preferred_element_type=jnp.float32)
    edge_input = sender_projected[sender] + receiver_projected[receiver] + edge_bias
    activation = jax.nn.silu(edge_input).astype(jnp.bfloat16)
    edge_out = jnp.dot(activation, edge_weight, preferred_element_type=jnp.float32)
    mesh_next = (mesh_mid.astype(jnp.float32) + jax.ops.segment_sum(edge_out, receiver, num_segments=MESH)).astype(jnp.bfloat16)
    incoming_gradient = jnp.dot(cotangent, edge_weight.T, preferred_element_type=jnp.float32)[receiver]
    edge_grad = (incoming_gradient * silu_slope(edge_input)).astype(jnp.bfloat16)
    grad_wide = edge_grad.astype(jnp.float32)
    by_receiver = jax.ops.segment_sum(grad_wide, receiver, num_segments=MESH).astype(jnp.bfloat16)
    by_sender = jax.ops.segment_sum(grad_wide, sender, num_segments=MESH).astype(jnp.bfloat16)
    mesh_grad = cotangent.astype(jnp.float32) + jnp.dot(by_receiver, receiver_weight.T, preferred_element_type=jnp.float32)
    mesh_grad = (mesh_grad + jnp.dot(by_sender, sender_weight.T, preferred_element_type=jnp.float32)).astype(jnp.bfloat16)
    return (mesh_next, mesh_grad)
```

```python
import functools

import jax
import jax.numpy as jnp
from jax import lax
from jax.experimental import pallas as pl
from jax.experimental.pallas import tpu as pltpu
from jax.sharding import PartitionSpec as P

BF = jnp.bfloat16
F32 = jnp.float32
OUTER = 4


def dot(a, b):
    return jnp.dot(a, b, preferred_element_type=F32)


def dot_t(a, b):
    return lax.dot_general(a, b, (((1,), (1,)), ((), ())), preferred_element_type=F32)


def sigmoid(v):
    return 0.5 * jnp.tanh(0.5 * v) + 0.5


def two_terms(v):
    high = v.astype(BF)
    low = (v - high.astype(F32)).astype(BF)
    return high, low


def picks(row, count, first=0):
    n = row.shape[1]
    place = lax.broadcasted_iota(jnp.int32, (count, n), 0) + first
    return (place == row).astype(F32)


def kernel(
    inner,
    cap,
    grid_hbm,
    slot_ref,
    mesh_hbm,
    target_ref,
    grid_weight_hbm,
    mesh_weight_hbm,
    link_bias_ref,
    link_weight_hbm,
    link_gain_ref,
    sender_ref,
    receiver_ref,
    halo_ref,
    sender_weight_hbm,
    receiver_weight_hbm,
    edge_bias_ref,
    edge_weight_hbm,
    cotangent_hbm,
    next_ref,
    grad_ref,
    grid,
    mesh,
    cotangent,
    grid_weight,
    mesh_weight,
    link_weight,
    sender_weight,
    receiver_weight,
    edge_weight,
    outbox,
    inbox,
    mesh_all,
    target_all,
    sums_out,
    sums_in,
    rows_out,
    rows_in,
    back_out,
    back_in,
    local_sem,
    grid_send,
    grid_recv,
    mesh_send,
    mesh_recv,
    target_send,
    target_recv,
    sums_send,
    sums_recv,
    rows_send,
    rows_recv,
    back_send,
    back_recv,
):
    group = lax.axis_index("groups")
    me = lax.axis_index("region")
    count = OUTER * inner
    z = me // inner
    w = me % inner
    width = inner * cap
    nodes = mesh.shape[0]
    halo = halo_ref.shape[1]
    edges = sender_ref.shape[1]
    near = edges - edges // 4
    has_lower = me > 0
    has_upper = me < count - 1

    loads = []
    for i, (source, target) in enumerate(
        (
            (grid_hbm, grid),
            (mesh_hbm, mesh),
            (grid_weight_hbm, grid_weight),
            (mesh_weight_hbm, mesh_weight),
            (link_weight_hbm, link_weight),
            (edge_weight_hbm, edge_weight),
            (cotangent_hbm, cotangent),
            (sender_weight_hbm, sender_weight),
            (receiver_weight_hbm, receiver_weight),
        )
    ):
        load = pltpu.make_async_copy(source, target, local_sem.at[i])
        load.start()
        loads.append(load)

    def signal(region):
        pl.semaphore_signal(
            barrier, inc=1, device_id=(group, region), device_id_type=pl.DeviceIdType.MESH
        )

    def send(source, target, send_sem, recv_sem, region):
        copy = pltpu.make_async_remote_copy(
            src_ref=source,
            dst_ref=target,
            send_sem=send_sem,
            recv_sem=recv_sem,
            device_id=(group, region),
            device_id_type=pl.DeviceIdType.MESH,
        )
        copy.start()
        return copy

    barrier = pltpu.get_barrier_semaphore()
    for step in range(1, OUTER):
        signal(lax.rem(z + step, OUTER) * inner + w)
    for step in range(1, inner):
        signal(z * inner + lax.rem(w + step, inner))

    @pl.when(has_lower)
    def _():
        signal(me - 1)

    @pl.when(has_upper)
    def _():
        signal(me + 1)

    steps = sorted(range(1, OUTER), key=lambda step: -min(step, OUTER - step)) + [0]

    def pack(step):
        first = lax.rem(z + step, OUTER) * width
        outbox[step] = dot(picks(slot_ref[...], width, first).astype(BF), grid[...]).astype(BF)

    loads[0].wait()
    pack(steps[0])
    rows_in[...] = jnp.zeros_like(rows_in)
    back_in[...] = jnp.zeros_like(back_in)
    pl.semaphore_wait(
        barrier, OUTER + inner - 2 + has_lower.astype(jnp.int32) + has_upper.astype(jnp.int32)
    )
    loads[1].wait()

    sent = []
    mesh_copies = {}
    target_copies = {}
    grid_copies = {}

    def send_grid(step):
        own = pl.ds(pl.multiple_of(w * cap, 16), cap)
        grid_copies[step] = []
        for turn in range(1, inner):
            other = lax.rem(w + turn, inner)
            grid_copies[step].append(
                send(
                    outbox.at[step, pl.ds(pl.multiple_of(other * cap, 16), cap)],
                    inbox.at[step, own],
                    grid_send.at[step, turn],
                    grid_recv.at[step, turn],
                    z * inner + other,
                )
            )
        inbox[step, own] = outbox[step, own]
        sent.extend(grid_copies[step])

    send_grid(steps[0])
    for step in steps[:-1]:
        back = OUTER - step
        other = lax.rem(z + back, OUTER)
        region = other * inner + w
        target_copies[step] = send(
            target_ref.at[:, pl.ds(pl.multiple_of(other * width, 128), width)],
            target_all.at[step],
            target_send.at[step],
            target_recv.at[step],
            region,
        )
        mesh_copies[step] = send(
            mesh, mesh_all.at[step], mesh_send.at[step], mesh_recv.at[step], region
        )
        sent.extend((target_copies[step], mesh_copies[step]))
    for step in steps[1:]:
        pack(step)
        send_grid(step)

    for load in loads[2:]:
        load.wait()
    high, low = two_terms(dot_t(cotangent[...], edge_weight[...]))
    incoming = jnp.concatenate([high, low], axis=0)

    total = None
    sums_copies = []
    for step in steps:
        for copy in grid_copies[step]:
            copy.wait_recv()
        if step:
            target_copies[step].wait_recv()
            mesh_copies[step].wait_recv()
            targets = target_all[step]
            latent = mesh_all[step]
        else:
            targets = target_ref[:, pl.ds(pl.multiple_of(z * width, 128), width)]
            latent = mesh[...]
        projected = dot(inbox[step], grid_weight[...]).astype(BF).astype(F32)
        high, low = two_terms(dot(latent, mesh_weight[...]) + link_bias_ref[...])
        table = jnp.concatenate([high, low], axis=0)
        part = None
        for edge in range(2):
            picker = picks(targets[edge : edge + 1], nodes)
            taker = picker.T.astype(BF)
            value = projected + dot(jnp.concatenate([taker, taker], axis=1), table)
            hidden = (value * sigmoid(value)).astype(BF)
            output = dot(hidden, link_weight[...])
            centred = output - jnp.mean(output, axis=-1, keepdims=True)
            spread = jnp.mean(centred * centred, axis=-1, keepdims=True)
            message = centred * lax.rsqrt(spread + 1e-05) * link_gain_ref[...]
            summed = dot(picker.astype(BF), message.astype(BF))
            part = summed if part is None else part + summed
        if step:
            sums_out[step] = part.astype(BF)
            copy = send(
                sums_out.at[step],
                sums_in.at[step],
                sums_send.at[step],
                sums_recv.at[step],
                lax.rem(z + step, OUTER) * inner + w,
            )
            sums_copies.append((step, copy))
            sent.append(copy)
        else:
            total = mesh[...].astype(F32) + part
    for step, copy in sums_copies:
        copy.wait_recv()
        total = total + sums_in[step].astype(F32)
    middle = total.astype(BF)

    def neighbour(source, target, send_sem, recv_sem):
        down = functools.partial(
            pltpu.make_async_remote_copy,
            src_ref=source.at[pl.ds(0, halo)],
            dst_ref=target.at[pl.ds(halo, halo)],
            send_sem=send_sem.at[0],
            recv_sem=recv_sem.at[0],
            device_id_type=pl.DeviceIdType.MESH,
        )
        up = functools.partial(
            pltpu.make_async_remote_copy,
            src_ref=source.at[pl.ds(halo, halo)],
            dst_ref=target.at[pl.ds(0, halo)],
            send_sem=send_sem.at[1],
            recv_sem=recv_sem.at[1],
            device_id_type=pl.DeviceIdType.MESH,
        )

        @pl.when(has_lower)
        def _():
            down(device_id=(group, me - 1)).start()

        @pl.when(has_upper)
        def _():
            up(device_id=(group, me + 1)).start()

        def arrive():
            @pl.when(has_upper)
            def _():
                down(device_id=(group, me - 1)).wait_recv()

            @pl.when(has_lower)
            def _():
                up(device_id=(group, me + 1)).wait_recv()

        def leave():
            @pl.when(has_lower)
            def _():
                down(device_id=(group, me - 1)).wait_send()

            @pl.when(has_upper)
            def _():
                up(device_id=(group, me + 1)).wait_send()

        return arrive, leave

    halo_picker = jnp.concatenate(
        [picks(halo_ref[0:1], nodes), picks(halo_ref[1:2], nodes)], axis=1
    )
    rows_out[...] = dot(halo_picker.T.astype(BF), middle).astype(BF)
    rows_arrive, rows_leave = neighbour(rows_out, rows_in, rows_send, rows_recv)

    senders = sender_ref[...]
    receivers = receiver_ref[...]
    receiver_picker = picks(receivers, nodes)
    receiver_taker = receiver_picker.T.astype(BF)
    receiver_taker = jnp.concatenate([receiver_taker, receiver_taker], axis=1)
    receiver_picker = receiver_picker.astype(BF)
    near_picker = picks(senders[:, :near], nodes)
    near_taker = near_picker.T.astype(BF)
    near_taker = jnp.concatenate([near_taker, near_taker], axis=1)
    far_picker = picks(senders[:, near:], 2 * halo, nodes)
    far_taker = far_picker.T.astype(BF)

    gradient = dot(receiver_taker, incoming)
    high, low = two_terms(dot(middle, receiver_weight[...]) + edge_bias_ref[...])
    receiver_part = dot(receiver_taker, jnp.concatenate([high, low], axis=0))
    high, low = two_terms(dot(middle, sender_weight[...]))
    near_input = receiver_part[:near] + dot(near_taker, jnp.concatenate([high, low], axis=0))

    def edge_values(value, slope):
        gate = sigmoid(value)
        active = (value * gate).astype(BF)
        back = (slope * (gate * (1.0 + value * (1.0 - gate)))).astype(BF)
        return active, back

    near_active, near_back = edge_values(near_input, gradient[:near])
    rows_arrive()
    high, low = two_terms(dot(rows_in[...], sender_weight[...]))
    far_input = receiver_part[near:] + dot(far_taker, high) + dot(far_taker, low)
    far_active, far_back = edge_values(far_input, gradient[near:])
    back_out[...] = dot(far_picker.astype(BF), far_back).astype(BF)
    back_arrive, back_leave = neighbour(back_out, back_in, back_send, back_recv)

    active_sum = dot(receiver_picker[:, :near], near_active) + dot(
        receiver_picker[:, near:], far_active
    )
    high, low = two_terms(active_sum)
    update = dot(high, edge_weight[...]) + dot(low, edge_weight[...])
    next_ref[...] = (middle.astype(F32) + update).astype(BF)
    by_receiver = dot(receiver_picker[:, :near], near_back) + dot(
        receiver_picker[:, near:], far_back
    )
    gradient_sum = cotangent[...].astype(F32) + dot_t(
        by_receiver.astype(BF), receiver_weight[...]
    )
    near_sum = dot(near_picker.astype(BF), near_back)
    back_arrive()
    by_sender = near_sum + dot(halo_picker.astype(BF), back_in[...])
    grad_ref[...] = (gradient_sum + dot_t(by_sender.astype(BF), sender_weight[...])).astype(BF)

    for copy in sent:
        copy.wait_send()
    rows_leave()
    back_leave()


def local(
    grid_latent,
    grid_slot,
    mesh_latent,
    link_target,
    grid_weight,
    mesh_weight,
    link_bias,
    link_weight,
    link_gain,
    edge_sender,
    edge_receiver,
    halo_list,
    sender_weight,
    receiver_weight,
    edge_bias,
    edge_weight,
    cotangent,
):
    regions = lax.axis_size("region")
    inner = regions // OUTER
    nodes, features = mesh_latent.shape
    halo = halo_list.shape[1]
    slots = link_target.shape[1]
    given = slots // regions
    cap = -(-given // 32) * 32
    if cap != given:
        grid_slot = grid_slot // given * cap + grid_slot % given
        link_target = jnp.pad(
            link_target.reshape(2, regions, given),
            ((0, 0), (0, 0), (0, cap - given)),
            constant_values=nodes,
        ).reshape(2, regions * cap)
    width = inner * cap
    vmem = pl.BlockSpec(memory_space=pltpu.VMEM)
    hbm = pl.BlockSpec(memory_space=pl.ANY)
    dma = pltpu.SemaphoreType.DMA
    square = pltpu.VMEM((features, features), BF)
    block = pltpu.VMEM((nodes, features), BF)
    return pl.pallas_call(
        functools.partial(kernel, inner, cap),
        out_shape=[jax.ShapeDtypeStruct((nodes, features), BF)] * 2,
        in_specs=[
            hbm, vmem, hbm, vmem, hbm, hbm, vmem, hbm, vmem,
            vmem, vmem, vmem, hbm, hbm, vmem, hbm, hbm,
        ],
        out_specs=[vmem, vmem],
        scratch_shapes=[
            pltpu.VMEM(grid_latent.shape, BF),
            block,
            block,
            square,
            square,
            square,
            square,
            square,
            square,
            pltpu.VMEM((OUTER, width, features), BF),
            pltpu.VMEM((OUTER, width, features), BF),
            pltpu.VMEM((OUTER, nodes, features), BF),
            pltpu.VMEM((OUTER, 2, width), jnp.int32),
            pltpu.VMEM((OUTER, nodes, features), BF),
            pltpu.VMEM((OUTER, nodes, features), BF),
            pltpu.VMEM((2 * halo, features), BF),
            pltpu.VMEM((2 * halo, features), BF),
            pltpu.VMEM((2 * halo, features), BF),
            pltpu.VMEM((2 * halo, features), BF),
            dma((9,)),
            dma((OUTER, inner)),
            dma((OUTER, inner)),
            dma((OUTER,)),
            dma((OUTER,)),
            dma((OUTER,)),
            dma((OUTER,)),
            dma((OUTER,)),
            dma((OUTER,)),
            dma((2,)),
            dma((2,)),
            dma((2,)),
            dma((2,)),
        ],
        compiler_params=pltpu.CompilerParams(
            collective_id=0, has_side_effects=True, vmem_limit_bytes=48 * 1024 * 1024
        ),
    )(
        grid_latent,
        grid_slot.reshape(1, -1),
        mesh_latent,
        link_target,
        grid_weight,
        mesh_weight,
        link_bias.reshape(1, -1),
        link_weight,
        link_gain.reshape(1, -1),
        edge_sender.reshape(1, -1),
        edge_receiver.reshape(1, -1),
        halo_list,
        sender_weight,
        receiver_weight,
        edge_bias.reshape(1, -1),
        edge_weight,
        cotangent,
    )


def solution(mesh):
    rows = P(("groups", "region"), None)
    line = P(("groups", "region"))
    return jax.shard_map(
        local,
        mesh=mesh,
        in_specs=(
            rows,
            line,
            rows,
            P(None, ("groups", "region")),
            P(),
            P(),
            P(),
            P(),
            P(),
            line,
            line,
            rows,
            P(),
            P(),
            P(),
            P(),
            rows,
        ),
        out_specs=(rows, rows),
        check_vma=False,
    )
```

```python
import functools

import jax
import jax.numpy as jnp
from jax import lax
from jax.experimental import pallas as pl
from jax.experimental.pallas import tpu as pltpu
from jax.sharding import PartitionSpec as P

BF = jnp.bfloat16
F32 = jnp.float32
OUTER = 4


def dot(a, b):
    return jnp.dot(a, b, preferred_element_type=F32)


def dot_t(a, b):
    return lax.dot_general(a, b, (((1,), (1,)), ((), ())), preferred_element_type=F32)


def sigmoid(v):
    return 0.5 * jnp.tanh(0.5 * v) + 0.5


def two_terms(v):
    high = v.astype(BF)
    low = (v - high.astype(F32)).astype(BF)
    return high, low


def picks(row, count, first=0):
    n = row.shape[1]
    place = lax.broadcasted_iota(jnp.int32, (count, n), 0) + first
    return (place == row).astype(F32)


def kernel(
    inner,
    cap,
    grid_hbm,
    slot_hbm,
    mesh_hbm,
    target_hbm,
    grid_weight_hbm,
    mesh_weight_hbm,
    link_bias_hbm,
    link_weight_hbm,
    link_gain_hbm,
    sender_hbm,
    receiver_hbm,
    halo_hbm,
    sender_weight_hbm,
    receiver_weight_hbm,
    edge_bias_hbm,
    edge_weight_hbm,
    cotangent_hbm,
    next_ref,
    grad_ref,
    grid,
    mesh,
    cotangent,
    grid_weight,
    mesh_weight,
    link_weight,
    sender_weight,
    receiver_weight,
    edge_weight,
    slot_ref,
    target_ref,
    link_bias_ref,
    link_gain_ref,
    sender_ref,
    receiver_ref,
    halo_ref,
    edge_bias_ref,
    outbox,
    inbox,
    mesh_all,
    target_all,
    sums_out,
    sums_in,
    rows_out,
    rows_in,
    back_out,
    back_in,
    local_sem,
    grid_send,
    grid_recv,
    mesh_send,
    mesh_recv,
    target_send,
    target_recv,
    sums_send,
    sums_recv,
    rows_send,
    rows_recv,
    back_send,
    back_recv,
):
    group = lax.axis_index("groups")
    me = lax.axis_index("region")
    count = OUTER * inner
    z = me // inner
    w = me % inner
    width = inner * cap
    nodes = mesh.shape[0]
    halo = halo_ref.shape[1]
    edges = sender_ref.shape[1]
    near = edges - edges // 4
    has_lower = me > 0
    has_upper = me < count - 1

    loads = []
    for i, (source, target) in enumerate(
        (
            (slot_hbm, slot_ref),
            (grid_hbm, grid),
            (mesh_hbm, mesh),
            (target_hbm, target_ref),
            (link_bias_hbm, link_bias_ref),
            (link_gain_hbm, link_gain_ref),
            (sender_hbm, sender_ref),
            (receiver_hbm, receiver_ref),
            (halo_hbm, halo_ref),
            (edge_bias_hbm, edge_bias_ref),
            (grid_weight_hbm, grid_weight),
            (mesh_weight_hbm, mesh_weight),
            (link_weight_hbm, link_weight),
            (edge_weight_hbm, edge_weight),
            (cotangent_hbm, cotangent),
            (sender_weight_hbm, sender_weight),
            (receiver_weight_hbm, receiver_weight),
        )
    ):
        load = pltpu.make_async_copy(source, target, local_sem.at[i])
        load.start()
        loads.append(load)

    def signal(region):
        pl.semaphore_signal(
            barrier, inc=1, device_id=(group, region), device_id_type=pl.DeviceIdType.MESH
        )

    def send(source, target, send_sem, recv_sem, region):
        copy = pltpu.make_async_remote_copy(
            src_ref=source,
            dst_ref=target,
            send_sem=send_sem,
            recv_sem=recv_sem,
            device_id=(group, region),
            device_id_type=pl.DeviceIdType.MESH,
        )
        copy.start()
        return copy

    barrier = pltpu.get_barrier_semaphore()
    for step in range(1, OUTER):
        signal(lax.rem(z + step, OUTER) * inner + w)
    for step in range(1, inner):
        signal(z * inner + lax.rem(w + step, inner))

    @pl.when(has_lower)
    def _():
        signal(me - 1)

    @pl.when(has_upper)
    def _():
        signal(me + 1)

    toward = 1 - 2 * (z // (OUTER // 2))

    def plane(step):
        return lax.rem(z + toward * (step + 1) + OUTER, OUTER)


    def pack(step):
        first = plane(step) * width
        outbox[step] = dot(picks(slot_ref[...], width, first).astype(BF), grid[...]).astype(BF)

    loads[0].wait()
    loads[1].wait()
    pack(0)
    rows_in[...] = jnp.zeros_like(rows_in)
    back_in[...] = jnp.zeros_like(back_in)
    pl.semaphore_wait(
        barrier, OUTER + inner - 2 + has_lower.astype(jnp.int32) + has_upper.astype(jnp.int32)
    )
    loads[2].wait()
    loads[3].wait()

    sent = []
    grid_copies = {}

    def send_grid(step):
        own = pl.ds(pl.multiple_of(w * cap, 16), cap)
        grid_copies[step] = []
        for turn in range(1, inner):
            other = lax.rem(w + turn, inner)
            grid_copies[step].append(
                send(
                    outbox.at[step, pl.ds(pl.multiple_of(other * cap, 16), cap)],
                    inbox.at[step, own],
                    grid_send.at[step, turn],
                    grid_recv.at[step, turn],
                    z * inner + other,
                )
            )
        inbox[step, own] = outbox[step, own]
        sent.extend(grid_copies[step])

    def mesh_copy(owner, up):
        return pltpu.make_async_remote_copy(
            src_ref=mesh_all.at[owner],
            dst_ref=mesh_all.at[owner],
            send_sem=mesh_send.at[up, owner],
            recv_sem=mesh_recv.at[owner],
            device_id=(group, (z + 2 * up - 1) * inner + w),
            device_id_type=pl.DeviceIdType.MESH,
        )

    def pass_on(owner, up):
        @pl.when(z < OUTER - 1 if up else z > 0)
        def _():
            mesh_copy(owner, up).start()

    def mesh_arrive(distance):
        @pl.when(z >= distance)
        def _():
            mesh_copy(z - distance, 1).wait_recv()
            pass_on(z - distance, 1)

        @pl.when(z + distance < OUTER)
        def _():
            mesh_copy(z + distance, 0).wait_recv()
            pass_on(z + distance, 0)

    def mesh_leave(distance):
        @pl.when((z >= distance) & (z < OUTER - 1))
        def _():
            mesh_copy(z - distance, 1).wait_send()

        @pl.when((z + distance < OUTER) & (z > 0))
        def _():
            mesh_copy(z + distance, 0).wait_send()

    mesh_all[z] = mesh[...]
    pass_on(z, 1)
    pass_on(z, 0)
    def target_copy(owner, region):
        return pltpu.make_async_remote_copy(
            src_ref=target_ref.at[
                :, pl.ds(pl.multiple_of((region // inner) * width, 128), width)
            ],
            dst_ref=target_all.at[owner],
            send_sem=target_send.at[region // inner],
            recv_sem=target_recv.at[owner],
            device_id=(group, region),
            device_id_type=pl.DeviceIdType.MESH,
        )

    def sums_copy(owner, other):
        return pltpu.make_async_remote_copy(
            src_ref=sums_out.at[other],
            dst_ref=sums_in.at[owner],
            send_sem=sums_send.at[other],
            recv_sem=sums_recv.at[owner],
            device_id=(group, other * inner + w),
            device_id_type=pl.DeviceIdType.MESH,
        )

    for step in range(OUTER - 1):
        copy = target_copy(z, plane(step) * inner + w)
        copy.start()
        sent.append(copy)
    send_grid(0)
    for step in range(1, OUTER):
        pack(step)
        send_grid(step)

    for load in loads[4:]:
        load.wait()
    high, low = two_terms(dot_t(cotangent[...], edge_weight[...]))
    incoming = jnp.concatenate([high, low], axis=0)

    total = None
    for step in range(OUTER):
        remote = step < OUTER - 1
        if remote:
            other = plane(step)
            mesh_arrive(step + 1)
            target_copy(other, other * inner + w).wait_recv()
            targets = target_all[other]
            latent = mesh_all[other]
        else:
            targets = target_ref[:, pl.ds(pl.multiple_of(z * width, 128), width)]
            latent = mesh[...]
        for copy in grid_copies[step]:
            copy.wait_recv()
        projected = dot(inbox[step], grid_weight[...]).astype(BF).astype(F32)
        high, low = two_terms(dot(latent, mesh_weight[...]) + link_bias_ref[...])
        table = jnp.concatenate([high, low], axis=0)
        part = None
        for edge in range(2):
            picker = picks(targets[edge : edge + 1], nodes)
            taker = picker.T.astype(BF)
            value = projected + dot(jnp.concatenate([taker, taker], axis=1), table)
            hidden = (value * sigmoid(value)).astype(BF)
            output = dot(hidden, link_weight[...])
            centred = output - jnp.mean(output, axis=-1, keepdims=True)
            spread = jnp.mean(centred * centred, axis=-1, keepdims=True)
            message = centred * lax.rsqrt(spread + 1e-05) * link_gain_ref[...]
            summed = dot(picker.astype(BF), message.astype(BF))
            part = summed if part is None else part + summed
        if remote:
            sums_out[other] = part.astype(BF)
            copy = sums_copy(z, other)
            copy.start()
            sent.append(copy)
        else:
            total = mesh[...].astype(F32) + part
    for step in range(OUTER - 1):
        other = plane(step)
        sums_copy(other, other).wait_recv()
        total = total + sums_in[other].astype(F32)
    middle = total.astype(BF)

    def neighbour(source, target, send_sem, recv_sem):
        down = functools.partial(
            pltpu.make_async_remote_copy,
            src_ref=source.at[pl.ds(0, halo)],
            dst_ref=target.at[pl.ds(halo, halo)],
            send_sem=send_sem.at[0],
            recv_sem=recv_sem.at[0],
            device_id_type=pl.DeviceIdType.MESH,
        )
        up = functools.partial(
            pltpu.make_async_remote_copy,
            src_ref=source.at[pl.ds(halo, halo)],
            dst_ref=target.at[pl.ds(0, halo)],
            send_sem=send_sem.at[1],
            recv_sem=recv_sem.at[1],
            device_id_type=pl.DeviceIdType.MESH,
        )

        @pl.when(has_lower)
        def _():
            down(device_id=(group, me - 1)).start()

        @pl.when(has_upper)
        def _():
            up(device_id=(group, me + 1)).start()

        def arrive():
            @pl.when(has_upper)
            def _():
                down(device_id=(group, me - 1)).wait_recv()

            @pl.when(has_lower)
            def _():
                up(device_id=(group, me + 1)).wait_recv()

        def leave():
            @pl.when(has_lower)
            def _():
                down(device_id=(group, me - 1)).wait_send()

            @pl.when(has_upper)
            def _():
                up(device_id=(group, me + 1)).wait_send()

        return arrive, leave

    halo_picker = jnp.concatenate(
        [picks(halo_ref[0:1], nodes), picks(halo_ref[1:2], nodes)], axis=1
    )
    rows_out[...] = dot(halo_picker.T.astype(BF), middle).astype(BF)
    rows_arrive, rows_leave = neighbour(rows_out, rows_in, rows_send, rows_recv)

    senders = sender_ref[...]
    receivers = receiver_ref[...]
    receiver_picker = picks(receivers, nodes)
    receiver_taker = receiver_picker.T.astype(BF)
    receiver_taker = jnp.concatenate([receiver_taker, receiver_taker], axis=1)
    receiver_picker = receiver_picker.astype(BF)
    near_picker = picks(senders[:, :near], nodes)
    near_taker = near_picker.T.astype(BF)
    near_taker = jnp.concatenate([near_taker, near_taker], axis=1)
    far_picker = picks(senders[:, near:], 2 * halo, nodes)
    far_taker = far_picker.T.astype(BF)

    gradient = dot(receiver_taker, incoming)
    high, low = two_terms(dot(middle, receiver_weight[...]) + edge_bias_ref[...])
    receiver_part = dot(receiver_taker, jnp.concatenate([high, low], axis=0))
    high, low = two_terms(dot(middle, sender_weight[...]))
    near_input = receiver_part[:near] + dot(near_taker, jnp.concatenate([high, low], axis=0))

    def edge_values(value, slope):
        gate = sigmoid(value)
        active = (value * gate).astype(BF)
        back = (slope * (gate * (1.0 + value * (1.0 - gate)))).astype(BF)
        return active, back

    near_active, near_back = edge_values(near_input, gradient[:near])
    rows_arrive()
    high, low = two_terms(dot(rows_in[...], sender_weight[...]))
    far_input = receiver_part[near:] + dot(far_taker, high) + dot(far_taker, low)
    far_active, far_back = edge_values(far_input, gradient[near:])
    back_out[...] = dot(far_picker.astype(BF), far_back).astype(BF)
    back_arrive, back_leave = neighbour(back_out, back_in, back_send, back_recv)

    active_sum = dot(receiver_picker[:, :near], near_active) + dot(
        receiver_picker[:, near:], far_active
    )
    high, low = two_terms(active_sum)
    update = dot(high, edge_weight[...]) + dot(low, edge_weight[...])
    next_ref[...] = (middle.astype(F32) + update).astype(BF)
    by_receiver = dot(receiver_picker[:, :near], near_back) + dot(
        receiver_picker[:, near:], far_back
    )
    gradient_sum = cotangent[...].astype(F32) + dot_t(
        by_receiver.astype(BF), receiver_weight[...]
    )
    near_sum = dot(near_picker.astype(BF), near_back)
    back_arrive()
    by_sender = near_sum + dot(halo_picker.astype(BF), back_in[...])
    grad_ref[...] = (gradient_sum + dot_t(by_sender.astype(BF), sender_weight[...])).astype(BF)

    for copy in sent:
        copy.wait_send()
    for step in range(OUTER - 1):
        mesh_leave(step)
    rows_leave()
    back_leave()


def local(
    grid_latent,
    grid_slot,
    mesh_latent,
    link_target,
    grid_weight,
    mesh_weight,
    link_bias,
    link_weight,
    link_gain,
    edge_sender,
    edge_receiver,
    halo_list,
    sender_weight,
    receiver_weight,
    edge_bias,
    edge_weight,
    cotangent,
):
    regions = lax.axis_size("region")
    inner = regions // OUTER
    nodes, features = mesh_latent.shape
    halo = halo_list.shape[1]
    slots = link_target.shape[1]
    given = slots // regions
    cap = -(-given // 32) * 32
    if cap != given:
        grid_slot = grid_slot // given * cap + grid_slot % given
        link_target = jnp.pad(
            link_target.reshape(2, regions, given),
            ((0, 0), (0, 0), (0, cap - given)),
            constant_values=nodes,
        ).reshape(2, regions * cap)
    width = inner * cap
    vmem = pl.BlockSpec(memory_space=pltpu.VMEM)
    hbm = pl.BlockSpec(memory_space=pltpu.HBM)
    dma = pltpu.SemaphoreType.DMA
    square = pltpu.VMEM((features, features), BF)
    block = pltpu.VMEM((nodes, features), BF)
    return pl.pallas_call(
        functools.partial(kernel, inner, cap),
        out_shape=[jax.ShapeDtypeStruct((nodes, features), BF)] * 2,
        in_specs=[hbm] * 17,
        out_specs=[vmem, vmem],
        scratch_shapes=[
            pltpu.VMEM(grid_latent.shape, BF),
            block,
            block,
            square,
            square,
            square,
            square,
            square,
            square,
            pltpu.VMEM((1, grid_slot.shape[0]), jnp.int32),
            pltpu.VMEM(link_target.shape, jnp.int32),
            pltpu.VMEM((1, features), F32),
            pltpu.VMEM((1, features), F32),
            pltpu.VMEM((1, edge_sender.shape[0]), jnp.int32),
            pltpu.VMEM((1, edge_sender.shape[0]), jnp.int32),
            pltpu.VMEM(halo_list.shape, jnp.int32),
            pltpu.VMEM((1, features), F32),
            pltpu.VMEM((OUTER, width, features), BF),
            pltpu.VMEM((OUTER, width, features), BF),
            pltpu.VMEM((OUTER, nodes, features), BF),
            pltpu.VMEM((OUTER, 2, width), jnp.int32),
            pltpu.VMEM((OUTER, nodes, features), BF),
            pltpu.VMEM((OUTER, nodes, features), BF),
            pltpu.VMEM((2 * halo, features), BF),
            pltpu.VMEM((2 * halo, features), BF),
            pltpu.VMEM((2 * halo, features), BF),
            pltpu.VMEM((2 * halo, features), BF),
            dma((17,)),
            dma((OUTER, inner)),
            dma((OUTER, inner)),
            dma((2, OUTER)),
            dma((OUTER,)),
            dma((OUTER,)),
            dma((OUTER,)),
            dma((OUTER,)),
            dma((OUTER,)),
            dma((2,)),
            dma((2,)),
            dma((2,)),
            dma((2,)),
        ],
        compiler_params=pltpu.CompilerParams(
            collective_id=0, has_side_effects=True, vmem_limit_bytes=60 * 1024 * 1024
        ),
    )(
        grid_latent,
        grid_slot.reshape(1, -1),
        mesh_latent,
        link_target,
        grid_weight,
        mesh_weight,
        link_bias.reshape(1, -1),
        link_weight,
        link_gain.reshape(1, -1),
        edge_sender.reshape(1, -1),
        edge_receiver.reshape(1, -1),
        halo_list,
        sender_weight,
        receiver_weight,
        edge_bias.reshape(1, -1),
        edge_weight,
        cotangent,
    )


def solution(mesh):
    rows = P(("groups", "region"), None)
    line = P(("groups", "region"))
    return jax.shard_map(
        local,
        mesh=mesh,
        in_specs=(
            rows,
            line,
            rows,
            P(None, ("groups", "region")),
            P(),
            P(),
            P(),
            P(),
            P(),
            line,
            line,
            rows,
            P(),
            P(),
            P(),
            P(),
            rows,
        ),
        out_specs=(rows, rows),
        check_vma=False,
    )
```

```python
import functools

import jax
import jax.numpy as jnp
from jax import lax
from jax.experimental import pallas as pl
from jax.experimental.pallas import tpu as pltpu
from jax.sharding import PartitionSpec as P

BF = jnp.bfloat16
F32 = jnp.float32
OUTER = 4


def dot(a, b):
    return jnp.dot(a, b, preferred_element_type=F32)


def dot_t(a, b):
    return lax.dot_general(a, b, (((1,), (1,)), ((), ())), preferred_element_type=F32)


def sigmoid(v):
    return 0.5 * jnp.tanh(0.5 * v) + 0.5


def two_terms(v):
    high = v.astype(BF)
    low = (v - high.astype(F32)).astype(BF)
    return high, low


def picks(row, count, first=0):
    n = row.shape[1]
    place = lax.broadcasted_iota(jnp.int32, (count, n), 0) + first
    return (place == row).astype(F32)


def kernel(
    inner,
    cap,
    grid_hbm,
    slot_hbm,
    mesh_hbm,
    target_hbm,
    grid_weight_hbm,
    mesh_weight_hbm,
    link_bias_hbm,
    link_weight_hbm,
    link_gain_hbm,
    sender_hbm,
    receiver_hbm,
    halo_hbm,
    sender_weight_hbm,
    receiver_weight_hbm,
    edge_bias_hbm,
    edge_weight_hbm,
    cotangent_hbm,
    both_ref,
    grid,
    mesh,
    cotangent,
    grid_weight,
    mesh_weight,
    link_weight,
    sender_weight,
    receiver_weight,
    edge_weight,
    slot_ref,
    target_ref,
    link_bias_ref,
    link_gain_ref,
    sender_ref,
    receiver_ref,
    halo_ref,
    edge_bias_ref,
    outbox,
    inbox,
    mesh_all,
    target_all,
    sums_out,
    sums_in,
    rows_out,
    rows_in,
    back_out,
    back_in,
    local_sem,
    grid_send,
    grid_recv,
    mesh_send,
    mesh_recv,
    target_send,
    target_recv,
    sums_send,
    sums_recv,
    rows_send,
    rows_recv,
    back_send,
    back_recv,
):
    group = lax.axis_index("groups")
    me = lax.axis_index("region")
    count = OUTER * inner
    z = me // inner
    w = me % inner
    width = inner * cap
    nodes = mesh.shape[0]
    halo = halo_ref.shape[1]
    edges = sender_ref.shape[1]
    near = edges - edges // 4
    has_lower = me > 0
    has_upper = me < count - 1

    loads = []
    for i, (source, target) in enumerate(
        (
            (slot_hbm, slot_ref),
            (grid_hbm, grid),
            (mesh_hbm, mesh),
            (target_hbm, target_ref),
            (link_bias_hbm, link_bias_ref),
            (link_gain_hbm, link_gain_ref),
            (sender_hbm, sender_ref),
            (receiver_hbm, receiver_ref),
            (halo_hbm, halo_ref),
            (edge_bias_hbm, edge_bias_ref),
            (grid_weight_hbm, grid_weight),
            (mesh_weight_hbm, mesh_weight),
            (link_weight_hbm, link_weight),
            (edge_weight_hbm, edge_weight),
            (cotangent_hbm, cotangent),
            (sender_weight_hbm, sender_weight),
            (receiver_weight_hbm, receiver_weight),
        )
    ):
        load = pltpu.make_async_copy(source, target, local_sem.at[i])
        load.start()
        loads.append(load)

    def signal(region):
        pl.semaphore_signal(
            barrier, inc=1, device_id=(group, region), device_id_type=pl.DeviceIdType.MESH
        )

    def send(source, target, send_sem, recv_sem, region):
        copy = pltpu.make_async_remote_copy(
            src_ref=source,
            dst_ref=target,
            send_sem=send_sem,
            recv_sem=recv_sem,
            device_id=(group, region),
            device_id_type=pl.DeviceIdType.MESH,
        )
        copy.start()
        return copy

    barrier = pltpu.get_barrier_semaphore()
    for step in range(1, OUTER):
        signal(lax.rem(z + step, OUTER) * inner + w)
    for step in range(1, inner):
        signal(z * inner + lax.rem(w + step, inner))

    @pl.when(has_lower)
    def _():
        signal(me - 1)

    @pl.when(has_upper)
    def _():
        signal(me + 1)

    turns = (lax.rem(z + 2, OUTER), 3 * lax.rem(z + 1, 2), 1 + lax.rem(z, 2), z)

    def plane(step):
        return turns[step]

    def pack(step):
        first = plane(step) * width
        outbox[step] = dot(picks(slot_ref[...], width, first).astype(BF), grid[...]).astype(BF)

    loads[0].wait()
    loads[1].wait()
    pack(0)
    rows_in[...] = jnp.zeros_like(rows_in)
    back_in[...] = jnp.zeros_like(back_in)
    pl.semaphore_wait(
        barrier, OUTER + inner - 2 + has_lower.astype(jnp.int32) + has_upper.astype(jnp.int32)
    )
    loads[2].wait()
    loads[3].wait()

    sent = []
    grid_copies = {}

    def send_grid(step):
        own = pl.ds(pl.multiple_of(w * cap, 16), cap)
        grid_copies[step] = []
        for turn in range(1, inner):
            other = lax.rem(w + turn, inner)
            grid_copies[step].append(
                send(
                    outbox.at[step, pl.ds(pl.multiple_of(other * cap, 16), cap)],
                    inbox.at[step, own],
                    grid_send.at[step, turn],
                    grid_recv.at[step, turn],
                    z * inner + other,
                )
            )
        inbox[step, own] = outbox[step, own]
        sent.extend(grid_copies[step])

    def mesh_copy(owner, up):
        return pltpu.make_async_remote_copy(
            src_ref=mesh_all.at[owner],
            dst_ref=mesh_all.at[owner],
            send_sem=mesh_send.at[up, owner],
            recv_sem=mesh_recv.at[owner],
            device_id=(group, (z + 2 * up - 1) * inner + w),
            device_id_type=pl.DeviceIdType.MESH,
        )

    def pass_on(owner, up):
        @pl.when(z < OUTER - 1 if up else z > 0)
        def _():
            mesh_copy(owner, up).start()

    def mesh_arrive(distance):
        @pl.when(z >= distance)
        def _():
            mesh_copy(z - distance, 1).wait_recv()
            pass_on(z - distance, 1)

        @pl.when(z + distance < OUTER)
        def _():
            mesh_copy(z + distance, 0).wait_recv()
            pass_on(z + distance, 0)

    def mesh_leave(distance):
        @pl.when((z >= distance) & (z < OUTER - 1))
        def _():
            mesh_copy(z - distance, 1).wait_send()

        @pl.when((z + distance < OUTER) & (z > 0))
        def _():
            mesh_copy(z + distance, 0).wait_send()

    mesh_all[z] = mesh[...]
    pass_on(z, 1)
    pass_on(z, 0)
    def target_copy(owner, region):
        return pltpu.make_async_remote_copy(
            src_ref=target_ref.at[
                :, pl.ds(pl.multiple_of((region // inner) * width, 128), width)
            ],
            dst_ref=target_all.at[owner],
            send_sem=target_send.at[region // inner],
            recv_sem=target_recv.at[owner],
            device_id=(group, region),
            device_id_type=pl.DeviceIdType.MESH,
        )

    def sums_copy(owner, other):
        return pltpu.make_async_remote_copy(
            src_ref=sums_out.at[other],
            dst_ref=sums_in.at[owner],
            send_sem=sums_send.at[other],
            recv_sem=sums_recv.at[owner],
            device_id=(group, other * inner + w),
            device_id_type=pl.DeviceIdType.MESH,
        )

    for step in range(OUTER - 1):
        copy = target_copy(z, plane(step) * inner + w)
        copy.start()
        sent.append(copy)
    send_grid(0)
    for step in range(1, OUTER):
        pack(step)
        send_grid(step)

    for load in loads[4:]:
        load.wait()
    high, low = two_terms(dot_t(cotangent[...], edge_weight[...]))
    incoming = jnp.concatenate([high, low], axis=0)

    halo_picker = jnp.concatenate(
        [picks(halo_ref[0:1], nodes), picks(halo_ref[1:2], nodes)], axis=1
    )
    halo_taker = halo_picker.T.astype(BF)
    halo_picker = halo_picker.astype(BF)
    senders = sender_ref[...]
    receivers = receiver_ref[...]
    receiver_picker = picks(receivers, nodes)
    receiver_taker = receiver_picker.T.astype(BF)
    receiver_taker = jnp.concatenate([receiver_taker, receiver_taker], axis=1)
    receiver_picker = receiver_picker.astype(BF)
    near_picker = picks(senders[:, :near], nodes)
    near_taker = near_picker.T.astype(BF)
    near_taker = jnp.concatenate([near_taker, near_taker], axis=1)
    far_picker = picks(senders[:, near:], 2 * halo, nodes)
    far_taker = far_picker.T.astype(BF)
    near_picker = near_picker.astype(BF)
    far_picker = far_picker.astype(BF)

    gradient = dot(receiver_taker, incoming)
    total = None
    for step in range(OUTER):
        remote = step < OUTER - 1
        if remote:
            other = plane(step)
            for distance in ((1, 2), (3,), ())[step]:
                mesh_arrive(distance)
            target_copy(other, other * inner + w).wait_recv()
            targets = target_all[other]
            latent = mesh_all[other]
        else:
            targets = target_ref[:, pl.ds(pl.multiple_of(z * width, 128), width)]
            latent = mesh[...]
        for copy in grid_copies[step]:
            copy.wait_recv()
        projected = dot(inbox[step], grid_weight[...]).astype(BF).astype(F32)
        high, low = two_terms(dot(latent, mesh_weight[...]) + link_bias_ref[...])
        table = jnp.concatenate([high, low], axis=0)
        part = None
        for edge in range(2):
            picker = picks(targets[edge : edge + 1], nodes)
            taker = picker.T.astype(BF)
            value = projected + dot(jnp.concatenate([taker, taker], axis=1), table)
            hidden = (value * sigmoid(value)).astype(BF)
            output = dot(hidden, link_weight[...])
            centred = output - jnp.mean(output, axis=-1, keepdims=True)
            spread = jnp.mean(centred * centred, axis=-1, keepdims=True)
            message = centred * lax.rsqrt(spread + 1e-05) * link_gain_ref[...]
            summed = dot(picker.astype(BF), message.astype(BF))
            part = summed if part is None else part + summed
        if remote:
            sums_out[other] = part.astype(BF)
            copy = sums_copy(z, other)
            copy.start()
            sent.append(copy)
        else:
            total = mesh[...].astype(F32) + part
    for step in range(OUTER - 1):
        other = plane(step)
        sums_copy(other, other).wait_recv()
        total = total + sums_in[other].astype(F32)
    middle = total.astype(BF)

    def neighbour(source, target, send_sem, recv_sem):
        down = functools.partial(
            pltpu.make_async_remote_copy,
            src_ref=source.at[pl.ds(0, halo)],
            dst_ref=target.at[pl.ds(halo, halo)],
            send_sem=send_sem.at[0],
            recv_sem=recv_sem.at[0],
            device_id_type=pl.DeviceIdType.MESH,
        )
        up = functools.partial(
            pltpu.make_async_remote_copy,
            src_ref=source.at[pl.ds(halo, halo)],
            dst_ref=target.at[pl.ds(0, halo)],
            send_sem=send_sem.at[1],
            recv_sem=recv_sem.at[1],
            device_id_type=pl.DeviceIdType.MESH,
        )

        @pl.when(has_lower)
        def _():
            down(device_id=(group, me - 1)).start()

        @pl.when(has_upper)
        def _():
            up(device_id=(group, me + 1)).start()

        def arrive():
            @pl.when(has_upper)
            def _():
                down(device_id=(group, me - 1)).wait_recv()

            @pl.when(has_lower)
            def _():
                up(device_id=(group, me + 1)).wait_recv()

        def leave():
            @pl.when(has_lower)
            def _():
                down(device_id=(group, me - 1)).wait_send()

            @pl.when(has_upper)
            def _():
                up(device_id=(group, me + 1)).wait_send()

        return arrive, leave

    rows_out[...] = dot(halo_taker, middle).astype(BF)
    rows_arrive, rows_leave = neighbour(rows_out, rows_in, rows_send, rows_recv)

    high, low = two_terms(dot(middle, receiver_weight[...]) + edge_bias_ref[...])
    receiver_part = dot(receiver_taker, jnp.concatenate([high, low], axis=0))
    high, low = two_terms(dot(middle, sender_weight[...]))
    near_input = receiver_part[:near] + dot(near_taker, jnp.concatenate([high, low], axis=0))

    def edge_values(value, slope):
        gate = sigmoid(value)
        active = (value * gate).astype(BF)
        back = (slope * (gate * (1.0 + value * (1.0 - gate)))).astype(BF)
        return active, back

    near_active, near_back = edge_values(near_input, gradient[:near])
    rows_arrive()
    high, low = two_terms(dot(rows_in[...], sender_weight[...]))
    far_input = receiver_part[near:] + dot(far_taker, high) + dot(far_taker, low)
    far_active, far_back = edge_values(far_input, gradient[near:])
    back_out[...] = dot(far_picker, far_back).astype(BF)
    back_arrive, back_leave = neighbour(back_out, back_in, back_send, back_recv)

    active_sum = dot(receiver_picker[:, :near], near_active) + dot(
        receiver_picker[:, near:], far_active
    )
    high, low = two_terms(active_sum)
    update = dot(high, edge_weight[...]) + dot(low, edge_weight[...])
    both_ref[0] = (middle.astype(F32) + update).astype(BF)
    by_receiver = dot(receiver_picker[:, :near], near_back) + dot(
        receiver_picker[:, near:], far_back
    )
    gradient_sum = cotangent[...].astype(F32) + dot_t(
        by_receiver.astype(BF), receiver_weight[...]
    )
    near_sum = dot(near_picker, near_back)
    back_arrive()
    by_sender = near_sum + dot(halo_picker, back_in[...])
    both_ref[1] = (gradient_sum + dot_t(by_sender.astype(BF), sender_weight[...])).astype(BF)

    for copy in sent:
        copy.wait_send()
    for step in range(OUTER - 1):
        mesh_leave(step)
    rows_leave()
    back_leave()


def local(
    grid_latent,
    grid_slot,
    mesh_latent,
    link_target,
    grid_weight,
    mesh_weight,
    link_bias,
    link_weight,
    link_gain,
    edge_sender,
    edge_receiver,
    halo_list,
    sender_weight,
    receiver_weight,
    edge_bias,
    edge_weight,
    cotangent,
):
    regions = lax.axis_size("region")
    inner = regions // OUTER
    nodes, features = mesh_latent.shape
    halo = halo_list.shape[1]
    slots = link_target.shape[1]
    given = slots // regions
    cap = -(-given // 32) * 32
    if cap != given:
        grid_slot = grid_slot // given * cap + grid_slot % given
        link_target = jnp.pad(
            link_target.reshape(2, regions, given),
            ((0, 0), (0, 0), (0, cap - given)),
            constant_values=nodes,
        ).reshape(2, regions * cap)
    width = inner * cap
    vmem = pl.BlockSpec(memory_space=pltpu.VMEM)
    hbm = pl.BlockSpec(memory_space=pltpu.HBM)
    dma = pltpu.SemaphoreType.DMA
    square = pltpu.VMEM((features, features), BF)
    block = pltpu.VMEM((nodes, features), BF)
    both = pl.pallas_call(
        functools.partial(kernel, inner, cap),
        out_shape=jax.ShapeDtypeStruct((2, nodes, features), BF),
        in_specs=[hbm] * 17,
        out_specs=vmem,
        scratch_shapes=[
            pltpu.VMEM(grid_latent.shape, BF),
            block,
            block,
            square,
            square,
            square,
            square,
            square,
            square,
            pltpu.VMEM((1, grid_slot.shape[0]), jnp.int32),
            pltpu.VMEM(link_target.shape, jnp.int32),
            pltpu.VMEM((1, features), F32),
            pltpu.VMEM((1, features), F32),
            pltpu.VMEM((1, edge_sender.shape[0]), jnp.int32),
            pltpu.VMEM((1, edge_sender.shape[0]), jnp.int32),
            pltpu.VMEM(halo_list.shape, jnp.int32),
            pltpu.VMEM((1, features), F32),
            pltpu.VMEM((OUTER, width, features), BF),
            pltpu.VMEM((OUTER, width, features), BF),
            pltpu.VMEM((OUTER, nodes, features), BF),
            pltpu.VMEM((OUTER, 2, width), jnp.int32),
            pltpu.VMEM((OUTER, nodes, features), BF),
            pltpu.VMEM((OUTER, nodes, features), BF),
            pltpu.VMEM((2 * halo, features), BF),
            pltpu.VMEM((2 * halo, features), BF),
            pltpu.VMEM((2 * halo, features), BF),
            pltpu.VMEM((2 * halo, features), BF),
            dma((17,)),
            dma((OUTER, inner)),
            dma((OUTER, inner)),
            dma((2, OUTER)),
            dma((OUTER,)),
            dma((OUTER,)),
            dma((OUTER,)),
            dma((OUTER,)),
            dma((OUTER,)),
            dma((2,)),
            dma((2,)),
            dma((2,)),
            dma((2,)),
        ],
        compiler_params=pltpu.CompilerParams(
            collective_id=0, has_side_effects=True, vmem_limit_bytes=60 * 1024 * 1024
        ),
    )(
        grid_latent,
        grid_slot.reshape(1, -1),
        mesh_latent,
        link_target,
        grid_weight,
        mesh_weight,
        link_bias.reshape(1, -1),
        link_weight,
        link_gain.reshape(1, -1),
        edge_sender.reshape(1, -1),
        edge_receiver.reshape(1, -1),
        halo_list,
        sender_weight,
        receiver_weight,
        edge_bias.reshape(1, -1),
        edge_weight,
        cotangent,
    )
    return both[0], both[1]


def solution(mesh):
    rows = P(("groups", "region"), None)
    line = P(("groups", "region"))
    return jax.shard_map(
        local,
        mesh=mesh,
        in_specs=(
            rows,
            line,
            rows,
            P(None, ("groups", "region")),
            P(),
            P(),
            P(),
            P(),
            P(),
            line,
            line,
            rows,
            P(),
            P(),
            P(),
            P(),
            rows,
        ),
        out_specs=(rows, rows),
        check_vma=False,
    )
```

```python
import functools

import jax
import jax.numpy as jnp
from jax import lax
from jax.experimental import pallas as pl
from jax.experimental.pallas import tpu as pltpu
from jax.sharding import PartitionSpec as P

BF = jnp.bfloat16
F32 = jnp.float32
OUTER = 4


def dot(a, b):
    return jnp.dot(a, b, preferred_element_type=F32)


def dot_t(a, b):
    return lax.dot_general(a, b, (((1,), (1,)), ((), ())), preferred_element_type=F32)


def sigmoid(v):
    return 0.5 * jnp.tanh(0.5 * v) + 0.5


def two_terms(v):
    high = v.astype(BF)
    low = (v - high.astype(F32)).astype(BF)
    return high, low


def picks(row, count, first=0):
    n = row.shape[1]
    place = lax.broadcasted_iota(jnp.int32, (count, n), 0) + first
    return (place == row).astype(F32)


def kernel(
    inner,
    cap,
    grid_hbm,
    slot_hbm,
    mesh_hbm,
    target_hbm,
    grid_weight_hbm,
    mesh_weight_hbm,
    link_bias_hbm,
    link_weight_hbm,
    link_gain_hbm,
    sender_hbm,
    receiver_hbm,
    halo_hbm,
    sender_weight_hbm,
    receiver_weight_hbm,
    edge_bias_hbm,
    edge_weight_hbm,
    cotangent_hbm,
    both_ref,
    grid,
    mesh,
    cotangent,
    grid_weight,
    mesh_weight,
    link_weight,
    sender_weight,
    receiver_weight,
    edge_weight,
    slot_ref,
    target_ref,
    link_bias_ref,
    link_gain_ref,
    sender_ref,
    receiver_ref,
    halo_ref,
    edge_bias_ref,
    outbox,
    inbox,
    mesh_all,
    target_all,
    sums_out,
    sums_in,
    rows_out,
    rows_in,
    back_out,
    back_in,
    local_sem,
    grid_send,
    grid_recv,
    mesh_send,
    mesh_recv,
    target_send,
    target_recv,
    sums_send,
    sums_recv,
    rows_send,
    rows_recv,
    back_send,
    back_recv,
):
    group = lax.axis_index("groups")
    me = lax.axis_index("region")
    count = OUTER * inner
    z = me // inner
    w = me % inner
    width = inner * cap
    nodes = mesh.shape[0]
    halo = halo_ref.shape[1]
    edges = sender_ref.shape[1]
    near = edges - edges // 4
    has_lower = me > 0
    has_upper = me < count - 1

    loads = []
    for i, (source, target) in enumerate(
        (
            (slot_hbm, slot_ref),
            (grid_hbm, grid),
            (mesh_hbm, mesh),
            (target_hbm, target_ref),
            (link_bias_hbm, link_bias_ref),
            (link_gain_hbm, link_gain_ref),
            (sender_hbm, sender_ref),
            (receiver_hbm, receiver_ref),
            (halo_hbm, halo_ref),
            (edge_bias_hbm, edge_bias_ref),
            (grid_weight_hbm, grid_weight),
            (mesh_weight_hbm, mesh_weight),
            (link_weight_hbm, link_weight),
            (edge_weight_hbm, edge_weight),
            (cotangent_hbm, cotangent),
            (sender_weight_hbm, sender_weight),
            (receiver_weight_hbm, receiver_weight),
        )
    ):
        load = pltpu.make_async_copy(source, target, local_sem.at[i])
        load.start()
        loads.append(load)

    def signal(region):
        pl.semaphore_signal(
            barrier, inc=1, device_id=(group, region), device_id_type=pl.DeviceIdType.MESH
        )

    def send(source, target, send_sem, recv_sem, region):
        copy = pltpu.make_async_remote_copy(
            src_ref=source,
            dst_ref=target,
            send_sem=send_sem,
            recv_sem=recv_sem,
            device_id=(group, region),
            device_id_type=pl.DeviceIdType.MESH,
        )
        copy.start()
        return copy

    barrier = pltpu.get_barrier_semaphore()
    for step in range(1, OUTER):
        signal(lax.rem(z + step, OUTER) * inner + w)
    for step in range(1, inner):
        signal(z * inner + lax.rem(w + step, inner))

    @pl.when(has_lower)
    def _():
        signal(me - 1)

    @pl.when(has_upper)
    def _():
        signal(me + 1)

    turns = (lax.rem(z + 2, OUTER), 3 * lax.rem(z + 1, 2), 1 + lax.rem(z, 2), z)

    def plane(step):
        return turns[step]

    def pack(step):
        first = plane(step) * width
        outbox[step] = dot(picks(slot_ref[...], width, first).astype(BF), grid[...]).astype(BF)

    loads[0].wait()
    loads[1].wait()
    pack(0)
    rows_in[...] = jnp.zeros_like(rows_in)
    back_in[...] = jnp.zeros_like(back_in)
    pl.semaphore_wait(
        barrier, OUTER + inner - 2 + has_lower.astype(jnp.int32) + has_upper.astype(jnp.int32)
    )
    loads[2].wait()
    loads[3].wait()

    sent = []
    grid_copies = {}

    def send_grid(step):
        own = pl.ds(pl.multiple_of(w * cap, 16), cap)
        grid_copies[step] = []
        for turn in range(1, inner):
            other = lax.rem(w + turn, inner)
            grid_copies[step].append(
                send(
                    outbox.at[step, pl.ds(pl.multiple_of(other * cap, 16), cap)],
                    inbox.at[step, own],
                    grid_send.at[step, turn],
                    grid_recv.at[step, w],
                    z * inner + other,
                )
            )
        inbox[step, own] = outbox[step, own]
        sent.extend(grid_copies[step])

    def mesh_copy(owner, up):
        return pltpu.make_async_remote_copy(
            src_ref=mesh_all.at[owner],
            dst_ref=mesh_all.at[owner],
            send_sem=mesh_send.at[up, owner],
            recv_sem=mesh_recv.at[owner],
            device_id=(group, (z + 2 * up - 1) * inner + w),
            device_id_type=pl.DeviceIdType.MESH,
        )

    def pass_on(owner, up):
        @pl.when(z < OUTER - 1 if up else z > 0)
        def _():
            mesh_copy(owner, up).start()

    def mesh_arrive(distance):
        @pl.when(z >= distance)
        def _():
            mesh_copy(z - distance, 1).wait_recv()
            pass_on(z - distance, 1)

        @pl.when(z + distance < OUTER)
        def _():
            mesh_copy(z + distance, 0).wait_recv()
            pass_on(z + distance, 0)

    def mesh_leave(distance):
        @pl.when((z >= distance) & (z < OUTER - 1))
        def _():
            mesh_copy(z - distance, 1).wait_send()

        @pl.when((z + distance < OUTER) & (z > 0))
        def _():
            mesh_copy(z + distance, 0).wait_send()

    mesh_all[z] = mesh[...]
    pass_on(z, 1)
    pass_on(z, 0)
    def target_copy(owner, region):
        return pltpu.make_async_remote_copy(
            src_ref=target_ref.at[
                :, pl.ds(pl.multiple_of((region // inner) * width, 128), width)
            ],
            dst_ref=target_all.at[owner],
            send_sem=target_send.at[region // inner],
            recv_sem=target_recv.at[owner],
            device_id=(group, region),
            device_id_type=pl.DeviceIdType.MESH,
        )

    def sums_copy(owner, other):
        return pltpu.make_async_remote_copy(
            src_ref=sums_out.at[other],
            dst_ref=sums_in.at[owner],
            send_sem=sums_send.at[other],
            recv_sem=sums_recv.at[owner],
            device_id=(group, other * inner + w),
            device_id_type=pl.DeviceIdType.MESH,
        )

    for step in range(OUTER - 1):
        copy = target_copy(z, plane(step) * inner + w)
        copy.start()
        sent.append(copy)
    send_grid(0)
    for step in range(1, OUTER):
        pack(step)
        send_grid(step)

    for load in loads[4:]:
        load.wait()
    high, low = two_terms(dot_t(cotangent[...], edge_weight[...]))
    incoming = jnp.concatenate([high, low], axis=0)

    halo_picker = jnp.concatenate(
        [picks(halo_ref[0:1], nodes), picks(halo_ref[1:2], nodes)], axis=1
    )
    halo_taker = halo_picker.T.astype(BF)
    halo_picker = halo_picker.astype(BF)
    senders = sender_ref[...]
    receivers = receiver_ref[...]
    receiver_picker = picks(receivers, nodes)
    receiver_taker = receiver_picker.T.astype(BF)
    receiver_taker = jnp.concatenate([receiver_taker, receiver_taker], axis=1)
    receiver_picker = receiver_picker.astype(BF)
    near_picker = picks(senders[:, :near], nodes)
    near_taker = near_picker.T.astype(BF)
    near_taker = jnp.concatenate([near_taker, near_taker], axis=1)
    far_picker = picks(senders[:, near:], 2 * halo, nodes)
    far_taker = far_picker.T.astype(BF)
    near_picker = near_picker.astype(BF)
    far_picker = far_picker.astype(BF)

    gradient = dot(receiver_taker, incoming)
    half = inner // 2
    side = w // half
    tables = {}

    def grid_arrive(step, owner):
        rows = pl.ds(pl.multiple_of(owner * cap, 16), cap)
        pltpu.make_async_remote_copy(
            src_ref=inbox.at[step, rows],
            dst_ref=inbox.at[step, rows],
            send_sem=grid_send.at[step, 0],
            recv_sem=grid_recv.at[step, owner],
            device_id=(group, me),
            device_id_type=pl.DeviceIdType.MESH,
        ).wait_recv()

    def plane_table(step):
        if step < OUTER - 1:
            other = plane(step)
            target_copy(other, other * inner + w).wait_recv()
            targets = target_all[other]
            latent = mesh_all[other]
        else:
            targets = target_ref[:, pl.ds(pl.multiple_of(z * width, 128), width)]
            latent = mesh[...]
        high, low = two_terms(dot(latent, mesh_weight[...]) + link_bias_ref[...])
        tables[step] = (jnp.concatenate([high, low], axis=0), targets)

    def link_sums(step, part):
        table, targets = tables[step]
        rows = half * cap
        targets = jnp.where(part == 0, targets[:, :rows], targets[:, rows:])
        taken = inbox[step, pl.ds(pl.multiple_of(part * rows, 16), rows)]
        projected = dot(taken, grid_weight[...]).astype(BF).astype(F32)
        total = None
        for edge in range(2):
            picker = picks(targets[edge : edge + 1], nodes)
            taker = picker.T.astype(BF)
            value = projected + dot(jnp.concatenate([taker, taker], axis=1), table)
            hidden = (value * sigmoid(value)).astype(BF)
            output = dot(hidden, link_weight[...])
            centred = output - jnp.mean(output, axis=-1, keepdims=True)
            spread = jnp.mean(centred * centred, axis=-1, keepdims=True)
            message = centred * lax.rsqrt(spread + 1e-05) * link_gain_ref[...]
            summed = dot(picker.astype(BF), message.astype(BF))
            total = summed if total is None else total + summed
        return total

    def near_half(step):
        plane_table(step)
        for turn in range(1, half):
            grid_arrive(step, side * half + lax.rem(lax.rem(w, half) + turn, half))
        return link_sums(step, side)

    def far_half(step):
        for turn in range(half):
            grid_arrive(step, (1 - side) * half + turn)
        return link_sums(step, 1 - side)

    def send_sums(step, part):
        other = plane(step)
        sums_out[other] = part.astype(BF)
        copy = sums_copy(z, other)
        copy.start()
        sent.append(copy)

    mesh_arrive(1)
    mesh_arrive(2)
    part = near_half(0)
    send_sums(0, part + far_half(0))
    mesh_arrive(3)
    part = near_half(1)
    send_sums(1, part + far_half(1))
    part = near_half(2)
    send_sums(2, part + far_half(2))
    part = near_half(3)
    total = mesh[...].astype(F32) + part + far_half(3)
    for step in range(OUTER - 1):
        other = plane(step)
        sums_copy(other, other).wait_recv()
        total = total + sums_in[other].astype(F32)
    middle = total.astype(BF)

    def neighbour(source, target, send_sem, recv_sem):
        down = functools.partial(
            pltpu.make_async_remote_copy,
            src_ref=source.at[pl.ds(0, halo)],
            dst_ref=target.at[pl.ds(halo, halo)],
            send_sem=send_sem.at[0],
            recv_sem=recv_sem.at[0],
            device_id_type=pl.DeviceIdType.MESH,
        )
        up = functools.partial(
            pltpu.make_async_remote_copy,
            src_ref=source.at[pl.ds(halo, halo)],
            dst_ref=target.at[pl.ds(0, halo)],
            send_sem=send_sem.at[1],
            recv_sem=recv_sem.at[1],
            device_id_type=pl.DeviceIdType.MESH,
        )

        @pl.when(has_lower)
        def _():
            down(device_id=(group, me - 1)).start()

        @pl.when(has_upper)
        def _():
            up(device_id=(group, me + 1)).start()

        def arrive():
            @pl.when(has_upper)
            def _():
                down(device_id=(group, me - 1)).wait_recv()

            @pl.when(has_lower)
            def _():
                up(device_id=(group, me + 1)).wait_recv()

        def leave():
            @pl.when(has_lower)
            def _():
                down(device_id=(group, me - 1)).wait_send()

            @pl.when(has_upper)
            def _():
                up(device_id=(group, me + 1)).wait_send()

        return arrive, leave

    rows_out[...] = dot(halo_taker, middle).astype(BF)
    rows_arrive, rows_leave = neighbour(rows_out, rows_in, rows_send, rows_recv)

    high, low = two_terms(dot(middle, receiver_weight[...]) + edge_bias_ref[...])
    receiver_part = dot(receiver_taker, jnp.concatenate([high, low], axis=0))
    high, low = two_terms(dot(middle, sender_weight[...]))
    near_input = receiver_part[:near] + dot(near_taker, jnp.concatenate([high, low], axis=0))

    def edge_values(value, slope):
        gate = sigmoid(value)
        active = (value * gate).astype(BF)
        back = (slope * (gate * (1.0 + value * (1.0 - gate)))).astype(BF)
        return active, back

    near_active, near_back = edge_values(near_input, gradient[:near])
    rows_arrive()
    high, low = two_terms(dot(rows_in[...], sender_weight[...]))
    far_input = receiver_part[near:] + dot(far_taker, high) + dot(far_taker, low)
    far_active, far_back = edge_values(far_input, gradient[near:])
    back_out[...] = dot(far_picker, far_back).astype(BF)
    back_arrive, back_leave = neighbour(back_out, back_in, back_send, back_recv)

    active_sum = dot(receiver_picker[:, :near], near_active) + dot(
        receiver_picker[:, near:], far_active
    )
    high, low = two_terms(active_sum)
    update = dot(high, edge_weight[...]) + dot(low, edge_weight[...])
    both_ref[0] = (middle.astype(F32) + update).astype(BF)
    by_receiver = dot(receiver_picker[:, :near], near_back) + dot(
        receiver_picker[:, near:], far_back
    )
    gradient_sum = cotangent[...].astype(F32) + dot_t(
        by_receiver.astype(BF), receiver_weight[...]
    )
    near_sum = dot(near_picker, near_back)
    back_arrive()
    by_sender = near_sum + dot(halo_picker, back_in[...])
    both_ref[1] = (gradient_sum + dot_t(by_sender.astype(BF), sender_weight[...])).astype(BF)

    for copy in sent:
        copy.wait_send()
    for step in range(OUTER - 1):
        mesh_leave(step)
    rows_leave()
    back_leave()


def local(
    grid_latent,
    grid_slot,
    mesh_latent,
    link_target,
    grid_weight,
    mesh_weight,
    link_bias,
    link_weight,
    link_gain,
    edge_sender,
    edge_receiver,
    halo_list,
    sender_weight,
    receiver_weight,
    edge_bias,
    edge_weight,
    cotangent,
):
    regions = lax.axis_size("region")
    inner = regions // OUTER
    nodes, features = mesh_latent.shape
    halo = halo_list.shape[1]
    slots = link_target.shape[1]
    given = slots // regions
    cap = -(-given // 32) * 32
    if cap != given:
        grid_slot = grid_slot // given * cap + grid_slot % given
        link_target = jnp.pad(
            link_target.reshape(2, regions, given),
            ((0, 0), (0, 0), (0, cap - given)),
            constant_values=nodes,
        ).reshape(2, regions * cap)
    width = inner * cap
    vmem = pl.BlockSpec(memory_space=pltpu.VMEM)
    hbm = pl.BlockSpec(memory_space=pltpu.HBM)
    dma = pltpu.SemaphoreType.DMA
    square = pltpu.VMEM((features, features), BF)
    block = pltpu.VMEM((nodes, features), BF)
    both = pl.pallas_call(
        functools.partial(kernel, inner, cap),
        out_shape=jax.ShapeDtypeStruct((2, nodes, features), BF),
        in_specs=[hbm] * 17,
        out_specs=vmem,
        scratch_shapes=[
            pltpu.VMEM(grid_latent.shape, BF),
            block,
            block,
            square,
            square,
            square,
            square,
            square,
            square,
            pltpu.VMEM((1, grid_slot.shape[0]), jnp.int32),
            pltpu.VMEM(link_target.shape, jnp.int32),
            pltpu.VMEM((1, features), F32),
            pltpu.VMEM((1, features), F32),
            pltpu.VMEM((1, edge_sender.shape[0]), jnp.int32),
            pltpu.VMEM((1, edge_sender.shape[0]), jnp.int32),
            pltpu.VMEM(halo_list.shape, jnp.int32),
            pltpu.VMEM((1, features), F32),
            pltpu.VMEM((OUTER, width, features), BF),
            pltpu.VMEM((OUTER, width, features), BF),
            pltpu.VMEM((OUTER, nodes, features), BF),
            pltpu.VMEM((OUTER, 2, width), jnp.int32),
            pltpu.VMEM((OUTER, nodes, features), BF),
            pltpu.VMEM((OUTER, nodes, features), BF),
            pltpu.VMEM((2 * halo, features), BF),
            pltpu.VMEM((2 * halo, features), BF),
            pltpu.VMEM((2 * halo, features), BF),
            pltpu.VMEM((2 * halo, features), BF),
            dma((17,)),
            dma((OUTER, inner)),
            dma((OUTER, inner)),
            dma((2, OUTER)),
            dma((OUTER,)),
            dma((OUTER,)),
            dma((OUTER,)),
            dma((OUTER,)),
            dma((OUTER,)),
            dma((2,)),
            dma((2,)),
            dma((2,)),
            dma((2,)),
        ],
        compiler_params=pltpu.CompilerParams(
            collective_id=0, has_side_effects=True, vmem_limit_bytes=60 * 1024 * 1024
        ),
    )(
        grid_latent,
        grid_slot.reshape(1, -1),
        mesh_latent,
        link_target,
        grid_weight,
        mesh_weight,
        link_bias.reshape(1, -1),
        link_weight,
        link_gain.reshape(1, -1),
        edge_sender.reshape(1, -1),
        edge_receiver.reshape(1, -1),
        halo_list,
        sender_weight,
        receiver_weight,
        edge_bias.reshape(1, -1),
        edge_weight,
        cotangent,
    )
    return both[0], both[1]


def solution(mesh):
    rows = P(("groups", "region"), None)
    line = P(("groups", "region"))
    return jax.shard_map(
        local,
        mesh=mesh,
        in_specs=(
            rows,
            line,
            rows,
            P(None, ("groups", "region")),
            P(),
            P(),
            P(),
            P(),
            P(),
            line,
            line,
            rows,
            P(),
            P(),
            P(),
            P(),
            rows,
        ),
        out_specs=(rows, rows),
        check_vma=False,
    )
```
